32 devices in a mesh: groups: 2 (over y), mp: 16 (over z, x, core).
Axes of the slice: x: 2, y: 2, z: 4, core: 2. Of those that a mesh axis runs over, the one named last changes fastest.
Arguments:
- residual: bfloat16 [256, 8192], P(('groups', 'mp')), parts along dimension 0, may hold values from -6 to 6
- prenorm_scale: float32 [8192], replicated, may hold values from 0.1 to 1.9
- gate_weight_matrix: bfloat16 [8192, 28672], P(None, 'mp'), may hold values from -0.0625 to 0.0625
- up_weight_matrix: bfloat16 [8192, 28672], P(None, 'mp'), may hold values from -0.0625 to 0.0625
- down_factor_weight: bfloat16 [32, 32, 8192], P('mp'), may hold values from -0.0625 to 0.0625
- up_factor_weight: bfloat16 [32, 32, 28672], P(None, None, 'mp'), may hold values from -1 to 1
- token_adapter_ids: int32 [256, 1], P('groups'), parts along dimension 0, may hold values from 0 to 31; in each aligned block of 128 rows (0 to 127, 128 to 255, ...) at most 8 rows name the same one
- adapter_store_rows: int32 [32], replicated, may hold values from 0 to 31, each once
Outputs:
- hidden: bfloat16 [256, 28672], P('groups', 'mp'), parts along dimension 0
The draws below stay inside these ranges and needn't reach their ends.
There are 2 independent parts, one for each index of `groups`. The reference program is written for one: setup_inputs(seed, part) draws one part's arguments, and reference() takes and returns one part's arrays. A program takes and returns all parts, laid end to end along the dimension named above; an argument that names none is the same for every part. Nothing has to cross between parts.
Inputs may be any that keep to these rules, and one draw needn't show every extreme that they name: `token_adapter_ids`: each adapter is named by at most 8 tokens of a replica, a bound that some block reaches. Each value appears once: adapter a's factors are row adapter_store_rows[a] of down_factor_weight and up_factor_weight.
All inputs are finite; a program needn't handle non-finite values.
Results may differ from the reference program's by a relative error of at most 0.0066.
Values may be sent and summed in bfloat16 or wider, within the bound.
A program may use at most 192 MiB of HBM per device.

```python
import math
import jax
import jax.numpy as jnp
import numpy as np
from jax import lax

MODEL_DIM = 8192
HIDDEN_DIM = 28672
ADAPTER_RANK = 16
ADAPTER_TOTAL = 32
TOKENS = 128
SEGMENT_SLOTS = 8


def steps_of(rng, extent, cuts, smallest, largest):
    loudness, own = 1.0, jax.random.fold_in(rng, 6)
    for dim, blocks in cuts:
        draws = jnp.exp(jax.random.uniform(jax.random.fold_in(own, dim), (blocks,), jnp.float32, smallest / len(cuts), largest / len(cuts)))
        loudness = loudness * jnp.repeat(draws, extent[dim] // blocks).reshape([-1 if axis == dim else 1 for axis in range(len(extent))])
    return loudness


def deal_out(rng, own, number, rows, count, top, bound, lean):
    sequence = jax.random.permutation(rng, count)
    packed, ordinary = shares(count, rows * top, bound, lean, True), shares(count, rows * top, bound, lean, False)
    places = jnp.arange(count)

    def named(sizes, turn):
        used = int((sizes > 0).sum())
        fixed = max(1, used // 4)
        moved = fixed + (places - fixed + turn * (used - fixed)) % max(1, count - fixed)
        return jnp.zeros((count,), jnp.int32).at[sequence[jnp.where(places < fixed, places, moved)]].set(jnp.asarray(sizes, jnp.int32))

    sizes = jnp.where(number % 4 == 0, named(packed, number // 4), named(ordinary, number - number // 4 - 1))
    mixed = jax.random.permutation(jax.random.fold_in(own, 3), count)
    giver, receiver = mixed[0:count // 2 * 2:2], mixed[1:count // 2 * 2:2]
    margin = jnp.minimum(sizes[giver] - 1, bound - sizes[receiver]) // 2
    margin = jnp.where((giver == sequence[0]) | (receiver == sequence[0]) | (sizes[receiver] == 0), 0, jnp.maximum(margin, 0))
    moved = jax.random.randint(jax.random.fold_in(own, 4), (count // 2,), 0, 1 << 20) % (margin + 1)
    sizes = sizes.at[giver].add(-moved).at[receiver].add(moved)
    members = jnp.searchsorted(jnp.cumsum(sizes), jnp.arange(rows * top), side="right").astype(jnp.int32)
    table = members.reshape(top, rows).T
    table = table[jax.random.permutation(jax.random.fold_in(own, 1), rows)]
    turn = jax.random.randint(jax.random.fold_in(own, 2), (rows, 1), 0, top)
    return jnp.take_along_axis(table, (jnp.arange(top)[None, :] + turn) % top, axis=1)


def shares(amount, total, most, lean, full):
    loads = [(1 << 20) // math.isqrt(standing ** lean) + 1 for standing in range(1, amount + 1)]
    largest = most if full else min(most, max(-(-total // amount), total * loads[0] // sum(loads)))
    least = 1 if total - largest >= amount - 1 else 0
    given, spare = [largest] + [least] * (amount - 1), total - largest - least * (amount - 1)
    while spare > 0:
        free = [i for i in range(1, amount) if given[i] < largest] or [i for i in range(1, amount) if given[i] < most]
        mass, remaining = sum([loads[i] for i in free]), spare
        for i in free:
            addition = min(most - given[i], max(1, remaining * loads[i] // mass), spare)
            given[i] = given[i] + addition
            spare = spare - addition
    return np.array(given)


def normal_values(own_key, extent, scale, limit, split=(), kind=jnp.bfloat16):
    result = jax.random.normal(own_key, extent, jnp.float32) * scale
    if len(split) > 0:
        result = steps_of(own_key, extent, split, -0.22, 0.18) * result
    return jnp.clip(result, min=-limit, max=limit).astype(kind)


def setup_inputs(seed: int = 0, part: int = 0) -> dict:
    streams_of = jax.random.split(jax.random.key(seed), 9)
    part_keys = jax.random.split(jax.random.fold_in(streams_of[8], part), 9)
    residual = normal_values(part_keys[0], (TOKENS, MODEL_DIM), 1.0, 6.0, ((0, 16),))
    prenorm_scale = jnp.clip(1.0 + 0.18 * jax.random.normal(streams_of[1], (MODEL_DIM,), jnp.float32), 0.1, 1.9)
    gate_weight_matrix = normal_values(streams_of[2], (MODEL_DIM, HIDDEN_DIM), MODEL_DIM ** -0.5, 0.0625, ((1, 16),))
    up_weight_matrix = normal_values(streams_of[3], (MODEL_DIM, HIDDEN_DIM), MODEL_DIM ** -0.5, 0.0625, ((1, 16),))
    down_factor_weight = normal_values(streams_of[4], (ADAPTER_TOTAL, 2 * ADAPTER_RANK, MODEL_DIM), MODEL_DIM ** -0.5, 0.0625, ((0, 16),))
    up_factor_weight = normal_values(streams_of[5], (ADAPTER_TOTAL, 2 * ADAPTER_RANK, HIDDEN_DIM), 0.125, 1.0, ((2, 16),))
    token_adapter_ids_keys = jax.random.split(jax.random.fold_in(part_keys[6], 1), TOKENS // TOKENS)
    token_adapter_ids_turns = jax.random.permutation(jax.random.fold_in(part_keys[6], 3), TOKENS // TOKENS)
    token_adapter_ids = jax.vmap(lambda own, number: deal_out(jax.random.fold_in(part_keys[6], 2), own, number, TOKENS, ADAPTER_TOTAL, 1, SEGMENT_SLOTS, 2))(token_adapter_ids_keys, token_adapter_ids_turns).reshape((TOKENS, 1))
    adapter_store_rows = jax.random.permutation(streams_of[7], ADAPTER_TOTAL).astype(jnp.int32)
    return {"residual": residual, "prenorm_scale": prenorm_scale, "gate_weight_matrix": gate_weight_matrix, "up_weight_matrix": up_weight_matrix, "down_factor_weight": down_factor_weight, "up_factor_weight": up_factor_weight, "token_adapter_ids": token_adapter_ids, "adapter_store_rows": adapter_store_rows}


ADAPTER_SCALE = 2.0

def slot_rows(token_adapter_ids, adapter_store_rows, capacity):
    slot_ids = adapter_store_rows[token_adapter_ids[:, 0]]
    adapter_list = adapter_store_rows.shape[0]
    onehot = (slot_ids[:, None] == jnp.arange(adapter_list, dtype=jnp.int32)[None, :]).astype(jnp.int32)
    earlier = jnp.cumsum(onehot, axis=0) - onehot
    within = lax.optimization_barrier(jnp.sum(earlier * onehot, axis=1))
    return (slot_ids * capacity + within).astype(jnp.int32)

def reference(residual, prenorm_scale, gate_weight_matrix, up_weight_matrix, down_factor_weight, up_factor_weight, token_adapter_ids, adapter_store_rows):
    widened = residual.astype(jnp.float32)
    rescale = lax.rsqrt(lax.optimization_barrier(jnp.mean(widened * widened, axis=1, keepdims=True)) + 1e-05)
    normalized_input = (widened * rescale * prenorm_scale).astype(jnp.bfloat16)
    store_row_index = slot_rows(token_adapter_ids, adapter_store_rows, SEGMENT_SLOTS)
    selected_factors = jnp.zeros((ADAPTER_TOTAL * SEGMENT_SLOTS, MODEL_DIM), jnp.bfloat16).at[store_row_index].set(normalized_input)
    reduced_tokens = jnp.einsum('unr,ugr->ung', selected_factors.reshape(ADAPTER_TOTAL, SEGMENT_SLOTS, MODEL_DIM).astype(jnp.float32), down_factor_weight.astype(jnp.float32)).astype(jnp.bfloat16)
    reduced_pair_rows = reduced_tokens.reshape(ADAPTER_TOTAL, SEGMENT_SLOTS, 2, ADAPTER_RANK).astype(jnp.float32)
    adapter_factors = up_factor_weight.reshape(ADAPTER_TOTAL, 2, ADAPTER_RANK, HIDDEN_DIM).astype(jnp.float32)
    adapter_correction = jnp.einsum('jyon,jonq->ojyq', reduced_pair_rows, adapter_factors).reshape(2, ADAPTER_TOTAL * SEGMENT_SLOTS, HIDDEN_DIM)
    gate_total_output = jnp.dot(normalized_input, gate_weight_matrix, preferred_element_type=jnp.float32) + ADAPTER_SCALE * adapter_correction[0][store_row_index]
    up_total_output = jnp.dot(normalized_input, up_weight_matrix, preferred_element_type=jnp.float32) + ADAPTER_SCALE * adapter_correction[1][store_row_index]
    return (jax.nn.silu(gate_total_output) * up_total_output).astype(jnp.bfloat16)
```

```python
import jax
import jax.numpy as jnp
from jax import lax
from jax.experimental import pallas as pl
from jax.experimental.pallas import tpu as pltpu
from jax.sharding import PartitionSpec as P

SEGMENT_SLOTS = 8
CHUNK = 1024
WIDE = 256
LINES = 4
LANES = 4
MESH = pl.DeviceIdType.MESH


ADAPTER_SCALE = 2.0


def slot_rows(token_adapter_ids, adapter_store_rows, capacity):
    slot_ids = adapter_store_rows[token_adapter_ids[:, 0]]
    adapter_list = adapter_store_rows.shape[0]
    onehot = (slot_ids[:, None] == jnp.arange(adapter_list, dtype=jnp.int32)[None, :]).astype(
        jnp.int32
    )
    earlier = jnp.cumsum(onehot, axis=0) - onehot
    within = jnp.sum(earlier * onehot, axis=1)
    return slot_ids * capacity + within


def on_device(
    residual,
    prenorm_scale,
    gate_weight_matrix,
    up_weight_matrix,
    down_factor_weight,
    up_factor_weight,
    token_adapter_ids,
    adapter_store_rows,
):
    widened = residual.astype(jnp.float32)
    rescale = lax.rsqrt(jnp.mean(widened * widened, axis=1, keepdims=True) + 1e-05)
    normalized_input = (widened * rescale * prenorm_scale).astype(jnp.bfloat16)
    store_row_index = slot_rows(token_adapter_ids, adapter_store_rows, SEGMENT_SLOTS)
    adapter_list = adapter_store_rows.shape[0]
    local_slot_rows = down_factor_weight.shape[0]
    reduced_width = down_factor_weight.shape[1]
    adapter_rank_size = reduced_width // 2
    hidden_model_width = down_factor_weight.shape[2]
    output_columns = gate_weight_matrix.shape[1]
    held_rows = local_slot_rows * SEGMENT_SLOTS
    targets = lax.axis_index("mp") * held_rows + jnp.arange(held_rows, dtype=jnp.int32)
    chooser = (store_row_index[None, :] == targets[:, None]).astype(jnp.bfloat16)
    gathered = lax.all_gather(normalized_input, "mp", axis=0, tiled=True)
    plain_gate_output = jnp.dot(gathered, gate_weight_matrix, preferred_element_type=jnp.float32)
    plain_up_output = jnp.dot(gathered, up_weight_matrix, preferred_element_type=jnp.float32)
    selected_factors = jnp.dot(chooser, gathered, preferred_element_type=jnp.float32).astype(
        jnp.bfloat16
    )
    reduced_tokens = jnp.einsum(
        "unr,ugr->ung",
        selected_factors.reshape(local_slot_rows, SEGMENT_SLOTS, hidden_model_width),
        down_factor_weight,
        preferred_element_type=jnp.float32,
    ).astype(jnp.bfloat16)
    flat_shrunk = reduced_tokens.reshape(held_rows * reduced_width)
    all_tokens_group = lax.all_gather(flat_shrunk, "mp", axis=0, tiled=True).reshape(
        adapter_list * SEGMENT_SLOTS, reduced_width
    )
    reduced_pair_rows = all_tokens_group.reshape(adapter_list, SEGMENT_SLOTS, 2, adapter_rank_size)
    adapter_factors = up_factor_weight.reshape(adapter_list, 2, adapter_rank_size, output_columns)
    adapter_correction = jnp.einsum(
        "jyon,jonq->ojyq", reduced_pair_rows, adapter_factors, preferred_element_type=jnp.float32
    ).reshape(2, adapter_list * SEGMENT_SLOTS, output_columns)
    gate_total_output = plain_gate_output + ADAPTER_SCALE * adapter_correction[0][store_row_index]
    up_total_output = plain_up_output + ADAPTER_SCALE * adapter_correction[1][store_row_index]
    return (jax.nn.silu(gate_total_output) * up_total_output).astype(jnp.bfloat16)


def supported(mesh, model, columns, adapters, tokens, rows, width):
    members = mesh.shape["mp"]
    return (
        members == LINES * LANES
        and tokens == members * rows
        and tokens == 128
        and rows == 8
        and model % CHUNK == 0
        and model // CHUNK >= 4
        and columns % 256 == 0
        and columns <= 2048
        and adapters == 2 * members
        and width == 32
    )


def fused_kernel(
    residual_hbm,
    scale_hbm,
    gate_hbm,
    up_hbm,
    down_hbm,
    factor_hbm,
    ids_hbm,
    rows_hbm,
    out_ref,
    residual,
    scale,
    ids,
    store_rows,
    down,
    factor,
    blocks,
    features,
    gate_ring,
    up_ring,
    gate_total,
    up_total,
    shrunk_total,
    shrunk_all,
    small_sem,
    down_sem,
    factor_sem,
    gate_sem,
    up_sem,
    z_send,
    z_recv,
    x_send,
    x_recv,
    c_send,
    c_recv,
    s_send,
    s_recv,
):
    members = LINES * LANES
    me = lax.axis_index("mp")
    z = me // 4
    x = (me // 2) % 2
    c = me % 2
    model = residual.shape[1]
    chunks = model // CHUNK
    half = CHUNK // 2
    columns = gate_hbm.shape[1]
    slots = gate_ring.shape[0]
    adapters = factor.shape[0]
    tokens = members * SEGMENT_SLOTS
    slot_total = adapters * SEGMENT_SLOTS
    f32, bf16 = jnp.float32, jnp.bfloat16

    def rows_of(i):
        return pl.ds(pl.multiple_of(i * CHUNK, CHUNK), CHUNK)

    def gate_copy(i):
        s = lax.rem(i, slots)
        return pltpu.make_async_copy(gate_hbm.at[rows_of(i)], gate_ring.at[s], gate_sem.at[s])

    def up_copy(i):
        s = lax.rem(i, slots)
        return pltpu.make_async_copy(up_hbm.at[rows_of(i)], up_ring.at[s], up_sem.at[s])

    small = [
        pltpu.make_async_copy(source, target, small_sem.at[k])
        for k, (source, target) in enumerate(
            ((residual_hbm, residual), (scale_hbm, scale), (ids_hbm, ids), (rows_hbm, store_rows))
        )
    ]
    for copy in small:
        copy.start()
    down_copy = pltpu.make_async_copy(down_hbm, down, down_sem)
    down_copy.start()
    factor_copy = pltpu.make_async_copy(factor_hbm, factor, factor_sem)

    barrier = pltpu.get_barrier_semaphore()

    @pl.loop(1, members)
    def _(k):
        pl.semaphore_signal(
            barrier, inc=1, device_id={"mp": lax.rem(me + k, members)}, device_id_type=MESH
        )

    @pl.loop(0, slots)
    def _(i):
        gate_copy(i).start()
        up_copy(i).start()

    factor_copy.start()

    small[0].wait()
    small[1].wait()
    wide = residual[...].astype(f32)
    rescale = lax.rsqrt(jnp.mean(wide * wide, axis=1, keepdims=True) + 1e-05)
    for i in range(chunks):
        first = slice(i * CHUNK, i * CHUNK + half)
        second = slice(i * CHUNK + half, (i + 1) * CHUNK)
        top = residual[:, first].astype(f32) * rescale * scale[:, first]
        bottom = residual[:, second].astype(f32) * rescale * scale[:, second]
        blocks[i, z, x, c] = jnp.concatenate([top, bottom], axis=0).astype(bf16)

    pl.semaphore_wait(barrier, members - 1)

    def z_copy(i, k):
        other = lax.rem(z + k, LINES)
        return pltpu.make_async_remote_copy(
            src_ref=blocks.at[i, z, x, c],
            dst_ref=blocks.at[i, z, x, c],
            send_sem=z_send.at[i, other],
            recv_sem=z_recv.at[i, z],
            device_id={"mp": other * LANES + x * 2 + c},
            device_id_type=MESH,
        )

    def z_arrival(i, k):
        other = lax.rem(z + k, LINES)
        return pltpu.make_async_remote_copy(
            src_ref=blocks.at[i, other, x, c],
            dst_ref=blocks.at[i, other, x, c],
            send_sem=z_send.at[i, other],
            recv_sem=z_recv.at[i, other],
            device_id={"mp": other * LANES + x * 2 + c},
            device_id_type=MESH,
        )

    def x_copy(i, lane):
        return pltpu.make_async_remote_copy(
            src_ref=blocks.at[i, :, lane, c],
            dst_ref=blocks.at[i, :, lane, c],
            send_sem=x_send.at[i],
            recv_sem=x_recv.at[i],
            device_id={"mp": z * LANES + (1 - x) * 2 + c},
            device_id_type=MESH,
        )

    def c_copy(i, core):
        return pltpu.make_async_remote_copy(
            src_ref=blocks.at[i, :, :, core],
            dst_ref=blocks.at[i, :, :, core],
            send_sem=c_send.at[i],
            recv_sem=c_recv.at[i],
            device_id={"mp": z * LANES + x * 2 + (1 - c)},
            device_id_type=MESH,
        )

    def s_copy(k):
        other = lax.rem(me + k, members)
        return pltpu.make_async_remote_copy(
            src_ref=shrunk_all.at[me],
            dst_ref=shrunk_all.at[me],
            send_sem=s_send.at[other],
            recv_sem=s_recv.at[me],
            device_id={"mp": other},
            device_id_type=MESH,
        )

    def s_arrival(k):
        other = lax.rem(me + k, members)
        return pltpu.make_async_remote_copy(
            src_ref=shrunk_all.at[other],
            dst_ref=shrunk_all.at[other],
            send_sem=s_send.at[other],
            recv_sem=s_recv.at[other],
            device_id={"mp": other},
            device_id_type=MESH,
        )

    @pl.loop(0, chunks)
    def _(i):
        for k in range(1, LINES):
            z_copy(i, k).start()

    gate_total[...] = jnp.zeros_like(gate_total)
    up_total[...] = jnp.zeros_like(up_total)
    shrunk_total[...] = jnp.zeros_like(shrunk_total)
    small[2].wait()
    small[3].wait()
    down_copy.wait()

    named = (lax.broadcasted_iota(jnp.int32, (adapters, tokens), 0) == ids[...]).astype(f32)
    stored = (lax.broadcasted_iota(jnp.int32, (adapters, adapters), 0) == store_rows[...]).astype(f32)
    in_slot = jnp.dot(stored.astype(bf16), named.astype(bf16), preferred_element_type=f32)
    before = (
        lax.broadcasted_iota(jnp.int32, (tokens, tokens), 0)
        < lax.broadcasted_iota(jnp.int32, (tokens, tokens), 1)
    ).astype(f32)
    earlier = jnp.dot(in_slot.astype(bf16), before.astype(bf16), preferred_element_type=f32)
    slot_number = lax.broadcasted_iota(jnp.int32, (adapters, tokens), 0).astype(f32)
    slot_row = jnp.sum(in_slot * (earlier + SEGMENT_SLOTS * slot_number), axis=0, keepdims=True)

    def gather_step(g):
        @pl.when(g < chunks)
        def _():
            for k in range(1, LINES):
                z_arrival(g, k).wait_recv()
            x_copy(g, x).start()

        @pl.when((g >= 1) & (g <= chunks))
        def _():
            x_copy(g - 1, 1 - x).wait_recv()
            c_copy(g - 1, c).start()

        @pl.when((g >= 2) & (g <= chunks + 1))
        def _():
            i = g - 2
            c_copy(i, 1 - c).wait_recv()
            taken = blocks[i].reshape(members, 16, half).astype(f32)
            for h in range(2):
                part = taken[:, h * 8 : (h + 1) * 8, :].reshape(tokens, half).astype(bf16)
                features[i, :, h * half : (h + 1) * half] = part
            factors = down[:, :, rows_of(i)].reshape(-1, CHUNK)
            shrunk_total[...] += lax.dot_general(
                features[i], factors, (((1,), (1,)), ((), ())), preferred_element_type=f32
            )

    def multiply(total, left, right_of):
        for j in range(columns // WIDE):
            cut = slice(j * WIDE, (j + 1) * WIDE)
            total[:, cut] += jnp.dot(left, right_of(cut), preferred_element_type=f32)

    def gate_step(i):
        gate_copy(i).wait()
        s = lax.rem(i, slots)
        multiply(gate_total, features[i], lambda cut: gate_ring[s, :, cut])

        @pl.when(i + slots < chunks)
        def _():
            gate_copy(i + slots).start()

    def up_step(i):
        up_copy(i).wait()
        s = lax.rem(i, slots)
        multiply(up_total, features[i], lambda cut: up_ring[s, :, cut])

        @pl.when(i + slots < chunks)
        def _():
            up_copy(i + slots).start()

    for g in range(3):
        gather_step(g)

    @pl.loop(0, chunks - 3)
    def _(i):
        gate_step(i)
        gather_step(3 + i + (i + 1) // 2)
        up_step(i)

        @pl.when(i % 2 == 0)
        def _():
            gather_step(4 + i + (i + 1) // 2)

    wanted = (me * 16 + lax.broadcasted_iota(jnp.int32, (16, tokens), 0)).astype(f32)
    chooser = (slot_row == wanted).astype(f32).astype(bf16)
    rounded = shrunk_total[...].astype(bf16)
    mine = jnp.dot(chooser, rounded, preferred_element_type=f32)
    row = lax.broadcasted_iota(jnp.int32, mine.shape, 0)
    lane = lax.broadcasted_iota(jnp.int32, mine.shape, 1)
    mine = jnp.where((row < 8) == (lane < 32), mine, 0.0)
    shrunk_all[me] = jnp.concatenate([mine, jnp.zeros_like(mine)], axis=1).astype(bf16)

    @pl.loop(1, members)
    def _(k):
        s_copy(k).start()

    @pl.loop(chunks - 3, chunks - 1)
    def _(i):
        gate_step(i)
        up_step(i)

    @pl.loop(1, members)
    def _(k):
        s_arrival(k).wait_recv()

    token_of = (
        lax.broadcasted_iota(jnp.int32, (slot_total, tokens), 0).astype(f32) == slot_row
    ).astype(f32)
    row_of = jnp.transpose(token_of).astype(bf16)
    gathered = shrunk_all[...].reshape(slot_total, 128)
    factor_copy.wait()
    spread_shape = (128, adapters * 16)
    for p, total in enumerate((gate_total, up_total)):
        lane = lax.broadcasted_iota(jnp.int32, spread_shape, 0)
        place = lax.broadcasted_iota(jnp.int32, spread_shape, 1)
        spreader = ((lane % 32 == p * 16 + place % 16) & (lane < 64)).astype(f32).astype(bf16)
        spread = jnp.dot(gathered, spreader, preferred_element_type=f32)
        owner = lax.broadcasted_iota(jnp.int32, spread.shape, 0) // SEGMENT_SLOTS
        place = lax.broadcasted_iota(jnp.int32, spread.shape, 1) // 16
        spread = jnp.where(owner == place, spread * ADAPTER_SCALE, 0.0).astype(bf16)
        left = jnp.dot(row_of, spread, preferred_element_type=f32).astype(bf16)
        multiply(
            total,
            left,
            lambda cut, p=p: factor[:, p * 16 : (p + 1) * 16, cut].reshape(adapters * 16, WIDE),
        )

    gate_step(chunks - 1)
    up_step(chunks - 1)
    for j in range(columns // WIDE):
        cut = slice(j * WIDE, (j + 1) * WIDE)
        value = gate_total[:, cut]
        out_ref[:, cut] = (value / (1.0 + jnp.exp(-value)) * up_total[:, cut]).astype(bf16)

    @pl.loop(0, chunks)
    def _(i):
        for k in range(1, LINES):
            z_copy(i, k).wait_send()
        x_copy(i, x).wait_send()
        c_copy(i, c).wait_send()

    @pl.loop(1, members)
    def _(k):
        s_copy(k).wait_send()


def fused(
    residual,
    prenorm_scale,
    gate_weight_matrix,
    up_weight_matrix,
    down_factor_weight,
    up_factor_weight,
    token_adapter_ids,
    adapter_store_rows,
):
    rows, model = residual.shape
    columns = gate_weight_matrix.shape[1]
    tokens = token_adapter_ids.shape[0]
    adapters = adapter_store_rows.shape[0]
    members = LINES * LANES
    chunks = model // CHUNK
    slots = min(6, chunks)
    half = CHUNK // 2
    bf16, f32 = jnp.bfloat16, jnp.float32
    anywhere = pl.BlockSpec(memory_space=pl.ANY)
    dma = pltpu.SemaphoreType.DMA
    return pl.pallas_call(
        fused_kernel,
        out_shape=jax.ShapeDtypeStruct((tokens, columns), bf16),
        in_specs=[anywhere] * 8,
        out_specs=pl.BlockSpec(memory_space=pltpu.VMEM),
        scratch_shapes=[
            pltpu.VMEM((rows, model), bf16),
            pltpu.VMEM((1, model), f32),
            pltpu.VMEM((1, tokens), jnp.int32),
            pltpu.VMEM((1, adapters), jnp.int32),
            pltpu.VMEM(down_factor_weight.shape, bf16),
            pltpu.VMEM(up_factor_weight.shape, bf16),
            pltpu.VMEM((chunks, LINES, 2, 2, 16, half), bf16),
            pltpu.VMEM((chunks, tokens, CHUNK), bf16),
            pltpu.VMEM((slots, CHUNK, columns), bf16),
            pltpu.VMEM((slots, CHUNK, columns), bf16),
            pltpu.VMEM((tokens, columns), f32),
            pltpu.VMEM((tokens, columns), f32),
            pltpu.VMEM((tokens, 64), f32),
            pltpu.VMEM((members, 16, 128), bf16),
            dma((4,)),
            dma,
            dma,
            dma((slots,)),
            dma((slots,)),
            dma((chunks, LINES)),
            dma((chunks, LINES)),
            dma((chunks,)),
            dma((chunks,)),
            dma((chunks,)),
            dma((chunks,)),
            dma((members,)),
            dma((members,)),
        ],
        compiler_params=pltpu.CompilerParams(
            collective_id=0, has_side_effects=True, vmem_limit_bytes=60 * 1024 * 1024
        ),
        cost_estimate=pl.CostEstimate(
            flops=4 * tokens * model * columns,
            bytes_accessed=4 * model * columns,
            transcendentals=tokens * columns,
        ),
    )(
        residual,
        prenorm_scale.reshape(1, model),
        gate_weight_matrix,
        up_weight_matrix,
        down_factor_weight,
        up_factor_weight,
        token_adapter_ids.reshape(1, tokens),
        adapter_store_rows.reshape(1, adapters),
    )


def solution(mesh):
    in_specs = (
        P(("groups", "mp"), None),
        P(),
        P(None, "mp"),
        P(None, "mp"),
        P("mp", None, None),
        P(None, None, "mp"),
        P("groups", None),
        P(),
    )
    out_specs = P("groups", "mp")

    def body(*args):
        residual, _, gate, _, down, _, ids, store = args
        rows, model = residual.shape
        fits = supported(
            mesh, model, gate.shape[1], store.shape[0], ids.shape[0], rows, down.shape[1]
        )
        return (fused if fits else on_device)(*args)

    return jax.shard_map(
        body, mesh=mesh, in_specs=in_specs, out_specs=out_specs, check_vma=False
    )
```

```python
import jax
import jax.numpy as jnp
from jax import lax
from jax.experimental import pallas as pl
from jax.experimental.pallas import tpu as pltpu
from jax.sharding import PartitionSpec as P

SEGMENT_SLOTS = 8
CHUNK = 1024
CORE_LAG = 2
USE_LAG = 3
AHEAD = 4
WIDE = 256
LINES = 4
LANES = 4
MESH = pl.DeviceIdType.MESH


ADAPTER_SCALE = 2.0


def slot_rows(token_adapter_ids, adapter_store_rows, capacity):
    slot_ids = adapter_store_rows[token_adapter_ids[:, 0]]
    adapter_list = adapter_store_rows.shape[0]
    onehot = (slot_ids[:, None] == jnp.arange(adapter_list, dtype=jnp.int32)[None, :]).astype(
        jnp.int32
    )
    earlier = jnp.cumsum(onehot, axis=0) - onehot
    within = jnp.sum(earlier * onehot, axis=1)
    return slot_ids * capacity + within


def on_device(
    residual,
    prenorm_scale,
    gate_weight_matrix,
    up_weight_matrix,
    down_factor_weight,
    up_factor_weight,
    token_adapter_ids,
    adapter_store_rows,
):
    widened = residual.astype(jnp.float32)
    rescale = lax.rsqrt(jnp.mean(widened * widened, axis=1, keepdims=True) + 1e-05)
    normalized_input = (widened * rescale * prenorm_scale).astype(jnp.bfloat16)
    store_row_index = slot_rows(token_adapter_ids, adapter_store_rows, SEGMENT_SLOTS)
    adapter_list = adapter_store_rows.shape[0]
    local_slot_rows = down_factor_weight.shape[0]
    reduced_width = down_factor_weight.shape[1]
    adapter_rank_size = reduced_width // 2
    hidden_model_width = down_factor_weight.shape[2]
    output_columns = gate_weight_matrix.shape[1]
    held_rows = local_slot_rows * SEGMENT_SLOTS
    targets = lax.axis_index("mp") * held_rows + jnp.arange(held_rows, dtype=jnp.int32)
    chooser = (store_row_index[None, :] == targets[:, None]).astype(jnp.bfloat16)
    gathered = lax.all_gather(normalized_input, "mp", axis=0, tiled=True)
    plain_gate_output = jnp.dot(gathered, gate_weight_matrix, preferred_element_type=jnp.float32)
    plain_up_output = jnp.dot(gathered, up_weight_matrix, preferred_element_type=jnp.float32)
    selected_factors = jnp.dot(chooser, gathered, preferred_element_type=jnp.float32).astype(
        jnp.bfloat16
    )
    reduced_tokens = jnp.einsum(
        "unr,ugr->ung",
        selected_factors.reshape(local_slot_rows, SEGMENT_SLOTS, hidden_model_width),
        down_factor_weight,
        preferred_element_type=jnp.float32,
    ).astype(jnp.bfloat16)
    flat_shrunk = reduced_tokens.reshape(held_rows * reduced_width)
    all_tokens_group = lax.all_gather(flat_shrunk, "mp", axis=0, tiled=True).reshape(
        adapter_list * SEGMENT_SLOTS, reduced_width
    )
    reduced_pair_rows = all_tokens_group.reshape(adapter_list, SEGMENT_SLOTS, 2, adapter_rank_size)
    adapter_factors = up_factor_weight.reshape(adapter_list, 2, adapter_rank_size, output_columns)
    adapter_correction = jnp.einsum(
        "jyon,jonq->ojyq", reduced_pair_rows, adapter_factors, preferred_element_type=jnp.float32
    ).reshape(2, adapter_list * SEGMENT_SLOTS, output_columns)
    gate_total_output = plain_gate_output + ADAPTER_SCALE * adapter_correction[0][store_row_index]
    up_total_output = plain_up_output + ADAPTER_SCALE * adapter_correction[1][store_row_index]
    return (jax.nn.silu(gate_total_output) * up_total_output).astype(jnp.bfloat16)


def supported(mesh, model, columns, adapters, tokens, rows, width):
    members = mesh.shape["mp"]
    return (
        members == LINES * LANES
        and tokens == members * rows
        and tokens == 128
        and rows == 8
        and model % CHUNK == 0
        and model // CHUNK >= 8
        and columns % 256 == 0
        and columns <= 2048
        and adapters == 2 * members
        and width == 32
    )


def fused_kernel(
    residual_hbm,
    scale_hbm,
    gate_hbm,
    up_hbm,
    down_hbm,
    factor_hbm,
    ids_hbm,
    rows_hbm,
    out_ref,
    residual,
    scale,
    ids,
    store_rows,
    down,
    factor,
    blocks,
    features,
    gate_ring,
    up_ring,
    gate_total,
    up_total,
    shrunk_total,
    shrunk_all,
    small_sem,
    down_sem,
    factor_sem,
    gate_sem,
    up_sem,
    z_send,
    z_recv,
    x_send,
    x_recv,
    c_send,
    c_recv,
    s_send,
    s_recv,
):
    members = LINES * LANES
    me = lax.axis_index("mp")
    z = me // 4
    x = (me // 2) % 2
    c = me % 2
    model = residual.shape[1]
    chunks = model // CHUNK
    half = CHUNK // 2
    columns = gate_hbm.shape[1]
    slots = gate_ring.shape[0]
    adapters = factor.shape[0]
    tokens = members * SEGMENT_SLOTS
    slot_total = adapters * SEGMENT_SLOTS
    f32, bf16 = jnp.float32, jnp.bfloat16

    def rows_of(i):
        return pl.ds(pl.multiple_of(i * CHUNK, CHUNK), CHUNK)

    def gate_copy(i):
        s = lax.rem(i, slots)
        return pltpu.make_async_copy(gate_hbm.at[rows_of(i)], gate_ring.at[s], gate_sem.at[s])

    def up_copy(i):
        s = lax.rem(i, slots)
        return pltpu.make_async_copy(up_hbm.at[rows_of(i)], up_ring.at[s], up_sem.at[s])

    small = [
        pltpu.make_async_copy(source, target, small_sem.at[k])
        for k, (source, target) in enumerate(
            ((residual_hbm, residual), (scale_hbm, scale), (ids_hbm, ids), (rows_hbm, store_rows))
        )
    ]
    for copy in small:
        copy.start()
    down_copy = pltpu.make_async_copy(down_hbm, down, down_sem)
    down_copy.start()
    factor_copy = pltpu.make_async_copy(factor_hbm, factor, factor_sem)

    barrier = pltpu.get_barrier_semaphore()

    @pl.loop(1, members)
    def _(k):
        pl.semaphore_signal(
            barrier, inc=1, device_id={"mp": lax.rem(me + k, members)}, device_id_type=MESH
        )

    @pl.loop(0, slots)
    def _(i):
        gate_copy(i).start()
        up_copy(i).start()

    factor_copy.start()

    small[0].wait()
    small[1].wait()
    wide = residual[...].astype(f32)
    rescale = lax.rsqrt(jnp.mean(wide * wide, axis=1, keepdims=True) + 1e-05)
    for i in range(chunks):
        first = slice(i * CHUNK, i * CHUNK + half)
        second = slice(i * CHUNK + half, (i + 1) * CHUNK)
        top = residual[:, first].astype(f32) * rescale * scale[:, first]
        bottom = residual[:, second].astype(f32) * rescale * scale[:, second]
        blocks[i, x, c, z] = jnp.concatenate([top, bottom], axis=0).astype(bf16)

    pl.semaphore_wait(barrier, members - 1)

    def z_copy(i, k):
        other = lax.rem(z + k, LINES)
        return pltpu.make_async_remote_copy(
            src_ref=blocks.at[i, x, c, z],
            dst_ref=blocks.at[i, x, c, z],
            send_sem=z_send.at[i, other],
            recv_sem=z_recv.at[i, z],
            device_id={"mp": other * LANES + x * 2 + c},
            device_id_type=MESH,
        )

    def z_arrival(i, k):
        other = lax.rem(z + k, LINES)
        return pltpu.make_async_remote_copy(
            src_ref=blocks.at[i, x, c, other],
            dst_ref=blocks.at[i, x, c, other],
            send_sem=z_send.at[i, other],
            recv_sem=z_recv.at[i, other],
            device_id={"mp": other * LANES + x * 2 + c},
            device_id_type=MESH,
        )

    def x_copy(i, lane):
        return pltpu.make_async_remote_copy(
            src_ref=blocks.at[i, lane, c],
            dst_ref=blocks.at[i, lane, c],
            send_sem=x_send.at[i],
            recv_sem=x_recv.at[i],
            device_id={"mp": z * LANES + (1 - x) * 2 + c},
            device_id_type=MESH,
        )

    def c_copy(i, core):
        return pltpu.make_async_remote_copy(
            src_ref=blocks.at[i, :, core],
            dst_ref=blocks.at[i, :, core],
            send_sem=c_send.at[i],
            recv_sem=c_recv.at[i],
            device_id={"mp": z * LANES + x * 2 + (1 - c)},
            device_id_type=MESH,
        )

    def s_copy(k):
        other = lax.rem(me + k, members)
        return pltpu.make_async_remote_copy(
            src_ref=shrunk_all.at[me],
            dst_ref=shrunk_all.at[me],
            send_sem=s_send.at[other],
            recv_sem=s_recv.at[me],
            device_id={"mp": other},
            device_id_type=MESH,
        )

    def s_arrival(k):
        other = lax.rem(me + k, members)
        return pltpu.make_async_remote_copy(
            src_ref=shrunk_all.at[other],
            dst_ref=shrunk_all.at[other],
            send_sem=s_send.at[other],
            recv_sem=s_recv.at[other],
            device_id={"mp": other},
            device_id_type=MESH,
        )

    @pl.loop(0, AHEAD)
    def _(i):
        for k in range(1, LINES):
            z_copy(i, k).start()

    gate_total[...] = jnp.zeros_like(gate_total)
    up_total[...] = jnp.zeros_like(up_total)
    shrunk_total[...] = jnp.zeros_like(shrunk_total)
    small[2].wait()
    small[3].wait()
    down_copy.wait()

    named = (lax.broadcasted_iota(jnp.int32, (adapters, tokens), 0) == ids[...]).astype(f32)
    stored = (lax.broadcasted_iota(jnp.int32, (adapters, adapters), 0) == store_rows[...]).astype(f32)
    in_slot = jnp.dot(stored.astype(bf16), named.astype(bf16), preferred_element_type=f32)
    before = (
        lax.broadcasted_iota(jnp.int32, (tokens, tokens), 0)
        < lax.broadcasted_iota(jnp.int32, (tokens, tokens), 1)
    ).astype(f32)
    earlier = jnp.dot(in_slot.astype(bf16), before.astype(bf16), preferred_element_type=f32)
    slot_number = lax.broadcasted_iota(jnp.int32, (adapters, tokens), 0).astype(f32)
    slot_row = jnp.sum(in_slot * (earlier + SEGMENT_SLOTS * slot_number), axis=0, keepdims=True)

    def gather_step(g):
        @pl.when(g + AHEAD < chunks)
        def _():
            for k in range(1, LINES):
                z_copy(g + AHEAD, k).start()

        @pl.when(g < chunks)
        def _():
            for k in range(1, LINES):
                z_arrival(g, k).wait_recv()
            x_copy(g, x).start()

        @pl.when((g >= CORE_LAG) & (g < chunks + CORE_LAG))
        def _():
            x_copy(g - CORE_LAG, 1 - x).wait_recv()
            c_copy(g - CORE_LAG, c).start()

        @pl.when((g >= USE_LAG) & (g < chunks + USE_LAG))
        def _():
            i = g - USE_LAG
            c_copy(i, 1 - c).wait_recv()
            places = [(a, b, d) for d in range(LINES) for a in range(2) for b in range(2)]
            taken = jnp.stack([blocks[i, a, b, d] for a, b, d in places]).astype(f32)
            for h in range(2):
                part = taken[:, h * 8 : (h + 1) * 8, :].reshape(tokens, half).astype(bf16)
                features[i, :, h * half : (h + 1) * half] = part
            factors = down[:, :, rows_of(i)].reshape(-1, CHUNK)
            shrunk_total[...] += lax.dot_general(
                features[i], factors, (((1,), (1,)), ((), ())), preferred_element_type=f32
            )

    def multiply(total, left, right_of):
        for j in range(columns // WIDE):
            cut = slice(j * WIDE, (j + 1) * WIDE)
            total[:, cut] += jnp.dot(left, right_of(cut), preferred_element_type=f32)

    def gate_step(i):
        gate_copy(i).wait()
        s = lax.rem(i, slots)
        multiply(gate_total, features[i], lambda cut: gate_ring[s, :, cut])

        @pl.when(i + slots < chunks)
        def _():
            gate_copy(i + slots).start()

    def up_step(i):
        up_copy(i).wait()
        s = lax.rem(i, slots)
        multiply(up_total, features[i], lambda cut: up_ring[s, :, cut])

        @pl.when(i + slots < chunks)
        def _():
            up_copy(i + slots).start()

    @pl.loop(0, USE_LAG + 1)
    def _(g):
        gather_step(g)

    @pl.loop(0, chunks - 1)
    def _(i):
        gate_step(i)
        gather_step(USE_LAG + 1 + i)
        up_step(i)

    wanted = (me * 16 + lax.broadcasted_iota(jnp.int32, (16, tokens), 0)).astype(f32)
    chooser = (slot_row == wanted).astype(f32).astype(bf16)
    rounded = shrunk_total[...].astype(bf16)
    mine = jnp.dot(chooser, rounded, preferred_element_type=f32)
    row = lax.broadcasted_iota(jnp.int32, mine.shape, 0)
    lane = lax.broadcasted_iota(jnp.int32, mine.shape, 1)
    mine = jnp.where((row < 8) == (lane < 32), mine, 0.0)
    shrunk_all[me] = jnp.concatenate([mine, jnp.zeros_like(mine)], axis=1).astype(bf16)

    @pl.loop(1, members)
    def _(k):
        s_copy(k).start()

    gate_step(chunks - 1)
    up_step(chunks - 1)

    @pl.loop(1, members)
    def _(k):
        s_arrival(k).wait_recv()

    token_of = (
        lax.broadcasted_iota(jnp.int32, (slot_total, tokens), 0).astype(f32) == slot_row
    ).astype(f32)
    row_of = jnp.transpose(token_of).astype(bf16)
    gathered = shrunk_all[...].reshape(slot_total, 128)
    factor_copy.wait()
    spread_shape = (128, adapters * 16)
    for p, total in enumerate((gate_total, up_total)):
        lane = lax.broadcasted_iota(jnp.int32, spread_shape, 0)
        place = lax.broadcasted_iota(jnp.int32, spread_shape, 1)
        spreader = ((lane % 32 == p * 16 + place % 16) & (lane < 64)).astype(f32).astype(bf16)
        spread = jnp.dot(gathered, spreader, preferred_element_type=f32)
        owner = lax.broadcasted_iota(jnp.int32, spread.shape, 0) // SEGMENT_SLOTS
        place = lax.broadcasted_iota(jnp.int32, spread.shape, 1) // 16
        spread = jnp.where(owner == place, spread * ADAPTER_SCALE, 0.0).astype(bf16)
        left = jnp.dot(row_of, spread, preferred_element_type=f32).astype(bf16)
        multiply(
            total,
            left,
            lambda cut, p=p: factor[:, p * 16 : (p + 1) * 16, cut].reshape(adapters * 16, WIDE),
        )

    for j in range(columns // WIDE):
        cut = slice(j * WIDE, (j + 1) * WIDE)
        value = gate_total[:, cut]
        out_ref[:, cut] = (value / (1.0 + jnp.exp(-value)) * up_total[:, cut]).astype(bf16)

    @pl.loop(0, chunks)
    def _(i):
        for k in range(1, LINES):
            z_copy(i, k).wait_send()
        x_copy(i, x).wait_send()
        c_copy(i, c).wait_send()

    @pl.loop(1, members)
    def _(k):
        s_copy(k).wait_send()


def fused(
    residual,
    prenorm_scale,
    gate_weight_matrix,
    up_weight_matrix,
    down_factor_weight,
    up_factor_weight,
    token_adapter_ids,
    adapter_store_rows,
):
    rows, model = residual.shape
    columns = gate_weight_matrix.shape[1]
    tokens = token_adapter_ids.shape[0]
    adapters = adapter_store_rows.shape[0]
    members = LINES * LANES
    chunks = model // CHUNK
    slots = min(6, chunks)
    half = CHUNK // 2
    bf16, f32 = jnp.bfloat16, jnp.float32
    anywhere = pl.BlockSpec(memory_space=pl.ANY)
    dma = pltpu.SemaphoreType.DMA
    return pl.pallas_call(
        fused_kernel,
        out_shape=jax.ShapeDtypeStruct((tokens, columns), bf16),
        in_specs=[anywhere] * 8,
        out_specs=pl.BlockSpec(memory_space=pltpu.VMEM),
        scratch_shapes=[
            pltpu.VMEM((rows, model), bf16),
            pltpu.VMEM((1, model), f32),
            pltpu.VMEM((1, tokens), jnp.int32),
            pltpu.VMEM((1, adapters), jnp.int32),
            pltpu.VMEM(down_factor_weight.shape, bf16),
            pltpu.VMEM(up_factor_weight.shape, bf16),
            pltpu.VMEM((chunks, 2, 2, LINES, 16, half), bf16),
            pltpu.VMEM((chunks, tokens, CHUNK), bf16),
            pltpu.VMEM((slots, CHUNK, columns), bf16),
            pltpu.VMEM((slots, CHUNK, columns), bf16),
            pltpu.VMEM((tokens, columns), f32),
            pltpu.VMEM((tokens, columns), f32),
            pltpu.VMEM((tokens, 64), f32),
            pltpu.VMEM((members, 16, 128), bf16),
            dma((4,)),
            dma,
            dma,
            dma((slots,)),
            dma((slots,)),
            dma((chunks, LINES)),
            dma((chunks, LINES)),
            dma((chunks,)),
            dma((chunks,)),
            dma((chunks,)),
            dma((chunks,)),
            dma((members,)),
            dma((members,)),
        ],
        compiler_params=pltpu.CompilerParams(
            collective_id=0, has_side_effects=True, vmem_limit_bytes=60 * 1024 * 1024
        ),
        cost_estimate=pl.CostEstimate(
            flops=4 * tokens * model * columns,
            bytes_accessed=4 * model * columns,
            transcendentals=tokens * columns,
        ),
    )(
        residual,
        prenorm_scale.reshape(1, model),
        gate_weight_matrix,
        up_weight_matrix,
        down_factor_weight,
        up_factor_weight,
        token_adapter_ids.reshape(1, tokens),
        adapter_store_rows.reshape(1, adapters),
    )


def solution(mesh):
    in_specs = (
        P(("groups", "mp"), None),
        P(),
        P(None, "mp"),
        P(None, "mp"),
        P("mp", None, None),
        P(None, None, "mp"),
        P("groups", None),
        P(),
    )
    out_specs = P("groups", "mp")

    def body(*args):
        residual, _, gate, _, down, _, ids, store = args
        rows, model = residual.shape
        fits = supported(
            mesh, model, gate.shape[1], store.shape[0], ids.shape[0], rows, down.shape[1]
        )
        return (fused if fits else on_device)(*args)

    return jax.shard_map(
        body, mesh=mesh, in_specs=in_specs, out_specs=out_specs, check_vma=False
    )
```
